256 devices in a mesh: section: 16 (over z, core), dp: 16 (over y, x).
Axes of the slice: x: 4, y: 4, z: 8, core: 2. Of those that a mesh axis runs over, the one named last changes fastest.
Arguments:
- master: float32 [256, 262144], P('section', 'dp'), may hold values from -6 to 6
- momentum: float32 [256, 262144], P('section', 'dp'), may hold values from -0.6 to 0.6
- variance: float32 [256, 262144], P('section', 'dp'), may hold values from 0.001 to 0.1
- grads: float32 [65536, 1024], P(('section', 'dp')), may hold values from -6 to 6
- counts: int32 [256], replicated, may hold values from 131072 to 262144
- old_layers: int32 [256], replicated, may hold values from 0 to 255, as said below
- new_layers: int32 [256], replicated, may hold values from 0 to 255, as said below
Outputs:
- new_master: float32 [65536, 1024], P(('section', 'dp'))
- new_momentum: float32 [65536, 1024], P(('section', 'dp'))
- new_variance: float32 [65536, 1024], P(('section', 'dp'))
- params: bfloat16 [65536, 1024], P(('section', 'dp'))
The draws below stay inside these ranges and needn't reach their ends.
Inputs may be any that keep to these rules, and one draw needn't show every extreme that they name: `old_layers`: a permutation of the layer ids. `new_layers`: a permutation of the layer ids; the 16 rows of each new section s (rows s * 16 to s * 16 + 15) hold exactly one layer from the rows of each old section j (rows j * 16 to j * 16 + 15 of old_layers), and that layer sits at row s * 16 + j.
All inputs are finite; a program needn't handle non-finite values.
Results may differ from the reference program's by a relative error of at most 0.001.
Values sent between devices are 32-bit elements; how exact they have to be, the bound alone decides.
No kernel may reach another device: no remote copies, remote signals or barrier semaphores. Data moves between devices by JAX's collectives and lax.ppermute only.
A program may use at most 64 MiB of HBM per device.

```python
import math
import jax
import jax.numpy as jnp

P_SIZE = 262144
STEP = 1000
LPS = 16
LAYERS = 256
N_DP = 16


def layer_plan(key):
    first_key, second_key, third_key = jax.random.split(key, 3)
    old_order = jax.random.permutation(first_key, LAYERS).astype(jnp.int32)
    group = LPS // N_DP
    dest_keys = jax.random.split(second_key, LPS)
    destination = jax.vmap(lambda k: jax.random.permutation(k, LPS))(dest_keys).astype(jnp.int32)
    slot_of = jnp.argsort(destination, axis=1).astype(jnp.int32)
    offset_keys = jax.random.split(third_key, LPS * N_DP)
    offsets = jax.vmap(lambda k: jax.random.permutation(k, group))(offset_keys).astype(jnp.int32)
    offsets = offsets.reshape(LPS, N_DP, group)
    section_ids = jnp.arange(LPS, dtype=jnp.int32)[:, None, None]
    group_ids = jnp.arange(N_DP, dtype=jnp.int32)[None, :, None]
    within_ids = jnp.arange(group, dtype=jnp.int32)[None, None, :]
    old_section = group_ids * group + within_ids
    target_row = section_ids * LPS + group_ids * group + offsets
    source_row = old_section * LPS + slot_of[old_section, section_ids]
    new_order = jnp.zeros((LAYERS,), jnp.int32).at[target_row.reshape(-1)].set(old_order[source_row.reshape(-1)])
    return (old_order, new_order)


def draw_old_layers(key, part):
    plan = layer_plan(key)
    return plan[0]


def draw_new_layers(key, part):
    plan = layer_plan(key)
    return plan[1]


def with_ends(array, key, least, top_value):
    spot = [jax.random.randint(jax.random.fold_in(key, axis), (), 0, length) for axis, length in enumerate(array.shape)]
    longest = array.shape.index(max(array.shape))
    beside = spot[:longest] + [(spot[longest] + 1) % array.shape[longest]] + spot[longest + 1:]
    return array.at[tuple(spot)].set(least).at[tuple(beside)].set(top_value)


def block_levels(rng, dims, pieces, smallest, largest):
    loudness = 1.0
    for dim, parts in pieces:
        draws = jax.random.uniform(jax.random.fold_in(jax.random.fold_in(rng, 6), dim), (parts,), jnp.float32, smallest / len(pieces), largest / len(pieces))
        loudness = loudness * jnp.repeat(jnp.exp(draws), dims[dim] // parts).reshape((-1,) + (1,) * (len(dims) - 1 - dim))
    return loudness


def bell_draw(rng, extent, scale, reach, cuts=(), held_as=jnp.bfloat16):
    entries = scale * jax.random.normal(rng, extent, jnp.float32)
    if cuts:
        entries = entries * block_levels(rng, extent, cuts, -0.22, 0.18)
    return jnp.clip(entries, -reach, reach).astype(held_as)


def setup_inputs(seed: int = 0) -> dict:
    splits = jax.random.split(jax.random.key(seed), 8)
    return {
        "master": bell_draw(splits[0], (LAYERS, P_SIZE), 1.0, 6.0, ((0, 16), (1, 16)), jnp.float32),
        "momentum": bell_draw(splits[1], (LAYERS, P_SIZE), 0.1, 0.6, ((0, 16), (1, 16)), jnp.float32),
        "variance": jnp.clip(jnp.exp(math.log(0.1) - 4.6051702 * jax.random.uniform(splits[2], (LAYERS, P_SIZE), jnp.float32) ** block_levels(splits[2], (LAYERS, P_SIZE), ((0, 16), (1, 16)), -0.2, 0.2)), 0.001, 0.1),
        "grads": bell_draw(splits[3], (LAYERS * P_SIZE // 1024, 1024), 1.0, 6.0, ((0, 256),), jnp.float32),
        "counts": with_ends(jax.random.randint(splits[4], (LAYERS,), P_SIZE // 2, P_SIZE + 1), jax.random.fold_in(splits[4], 1), P_SIZE // 2, P_SIZE).astype(jnp.int32),
        "old_layers": draw_old_layers(jax.random.fold_in(splits[7], 71), 0),
        "new_layers": draw_new_layers(jax.random.fold_in(splits[7], 71), 0),
    }


def reference(master, momentum, variance, grads, counts, old_layers, new_layers):
    total = old_layers.shape[0]
    width = master.shape[1]
    where_old = jnp.zeros((total,), jnp.int32).at[old_layers].set(jnp.arange(total, dtype=jnp.int32))
    source = where_old[new_layers]
    moved_master = master[source]
    moved_momentum = momentum[source]
    moved_variance = variance[source]
    grad = grads.reshape(total, width)
    limit = counts[new_layers]
    live = jnp.arange(width, dtype=jnp.int32)[None, :] < limit[:, None]
    first = 0.9 * moved_momentum + 0.1 * grad
    second = 0.95 * moved_variance + 0.05 * grad * grad
    step_size = first / (1.0 - 0.9 ** STEP) / (jnp.sqrt(second / (1.0 - 0.95 ** STEP)) + 1e-08)
    weight = moved_master - 0.01 * (step_size + 0.1 * moved_master)
    weight = jnp.where(live, weight, jnp.float32(0.0)).reshape(-1, 1024)
    first = jnp.where(live, first, jnp.float32(0.0)).reshape(-1, 1024)
    second = jnp.where(live, second, jnp.float32(0.0)).reshape(-1, 1024)
    return (weight, first, second, weight.astype(jnp.bfloat16))
```

```python
import functools

import jax
import jax.numpy as jnp
from jax import lax
from jax.experimental import pallas as pl
from jax.experimental.pallas import tpu as pltpu
from jax.sharding import PartitionSpec as P

STEP = 1000
LANES = 128
SUBLANES = 8
AXES = ("section", "dp")
ROUNDS = ((0, 0), (2, 0), (1, 0), (3, 0), (0, 1), (2, 1), (1, 1), (3, 1))
FIRST_SWAP = 6


def target(old_section, block, shift, flip):
    z, core = old_section >> 1, old_section & 1
    y, x = block >> 2, block & 3
    turn = 2 * ((y + shift) & 3) + ((x & 1) ^ flip)
    odd = (z & 1) ^ core
    move = (turn + odd * (4 - 2 * turn)) * (1 - 2 * core)
    return 2 * ((z + move) & 7) + (core ^ (x >> 1))


def origin(old_section, new_section, shift, flip):
    z, core = old_section >> 1, old_section & 1
    move = ((new_section >> 1) - z) * (1 - 2 * core)
    odd = (z & 1) ^ core
    turn = (move + odd * (4 - 2 * move)) & 7
    y = ((turn >> 1) - shift) & 3
    x = 2 * (core ^ (new_section & 1)) + ((turn & 1) ^ flip)
    return 4 * y + x


def round_pairs(shift, flip):
    pairs = []
    for section in range(16):
        for rank in range(16):
            there = target(section, rank, shift, flip)
            pairs.append((section * 16 + rank, there * 16 + section))
    return pairs


SWAP = [(s * 16 + r, (s ^ 1) * 16 + r) for s in range(16) for r in range(16)]


def pack_kernel(slots, old_ref, new_ref, *refs):
    states, messages = refs[:3], refs[3 : 3 + len(ROUNDS)]
    row_of, tiles = refs[3 + len(ROUNDS)], refs[4 + len(ROUNDS) :]
    section, rank = lax.axis_index("section"), lax.axis_index("dp")
    columns = states[0].shape[1] // LANES
    for slot in range(slots):
        row_of[old_ref[section * slots + slot]] = slot
    for state, tile in zip(states, tiles):
        for half in range(slots // SUBLANES):
            for column in range(columns):
                tile[pl.ds((half * columns + column) * SUBLANES, SUBLANES), :] = state[
                    pl.ds(half * SUBLANES, SUBLANES), pl.ds(column * LANES, LANES)
                ]
    for message, (shift, flip) in zip(messages, ROUNDS):
        there = target(section, rank, shift, flip)
        for part in range(2):
            row = row_of[new_ref[(there ^ part) * slots + section]]
            start = (row >> 3) * (columns * SUBLANES) + (row & 7)
            for index, tile in enumerate(tiles):
                for half in range(2):
                    for column in range(8):
                        message[
                            pl.ds((part * 3 + index) * 16 + half * SUBLANES, SUBLANES),
                            pl.ds(column * LANES, LANES),
                        ] = tile[
                            pl.ds(start + (64 * half + column) * SUBLANES, SUBLANES, stride=64), :
                        ]


def adamw(weight, first, second, grad, live):
    first = 0.9 * first + 0.1 * grad
    second = 0.95 * second + 0.05 * grad * grad
    step_size = first / (1.0 - 0.9**STEP) / (jnp.sqrt(second / (1.0 - 0.95**STEP)) + 1e-08)
    weight = weight - 0.01 * (step_size + 0.1 * weight)
    zero = jnp.float32(0.0)
    return (
        jnp.where(live, weight, zero),
        jnp.where(live, first, zero),
        jnp.where(live, second, zero),
    )


def update_kernel(slots, counts_ref, new_ref, grads, *refs):
    kept, swapped = refs[: len(ROUNDS)], refs[len(ROUNDS) : len(ROUNDS) + 2]
    outs = refs[len(ROUNDS) + 2 :]
    section, rank = lax.axis_index("section"), lax.axis_index("dp")
    limit = counts_ref[new_ref[section * slots + rank]]
    width = grads.shape[1]
    place = width * lax.broadcasted_iota(jnp.int32, (16, width), 0) + lax.broadcasted_iota(
        jnp.int32, (16, width), 1
    )
    for number, (shift, flip) in enumerate(ROUNDS):
        block = origin(rank, section, shift, flip)
        if number < FIRST_SWAP:
            other = swapped[0].at[pl.ds(48 * number, 48)]
        else:
            other = swapped[1].at[pl.ds(48 * (number - FIRST_SWAP), 48)]
        for held, spot in ((kept[number], block), (other, block ^ 2)):
            rows = pl.ds(pl.multiple_of(spot * 16, 16), 16)
            live = place < limit - spot * (16 * width)
            weight, first, second = adamw(
                held[pl.ds(0, 16), :], held[pl.ds(16, 16), :], held[pl.ds(32, 16), :], grads[rows, :], live
            )
            outs[0][rows, :] = weight
            outs[1][rows, :] = first
            outs[2][rows, :] = second
            outs[3][rows, :] = weight.astype(jnp.bfloat16)


def on_device(master, momentum, variance, grads, counts, old_layers, new_layers):
    slots, columns = master.shape
    vmem = pl.BlockSpec(memory_space=pltpu.VMEM)
    smem = pl.BlockSpec(memory_space=pltpu.SMEM)
    params = pltpu.CompilerParams(vmem_limit_bytes=40 * 2**20)
    messages = pl.pallas_call(
        functools.partial(pack_kernel, slots),
        out_shape=[jax.ShapeDtypeStruct((96, 1024), jnp.float32)] * len(ROUNDS),
        in_specs=[smem, smem, vmem, vmem, vmem],
        out_specs=[vmem] * len(ROUNDS),
        scratch_shapes=[pltpu.SMEM((old_layers.shape[0],), jnp.int32)]
        + [pltpu.VMEM((slots * columns // LANES, LANES), jnp.float32)] * 3,
        compiler_params=params,
    )(old_layers, new_layers, master, momentum, variance)
    arrived = [
        lax.ppermute(message, AXES, round_pairs(*turn)) for message, turn in zip(messages, ROUNDS)
    ]
    swapped = [
        lax.ppermute(jnp.concatenate([got[48:] for got in group]), AXES, SWAP)
        for group in (arrived[:FIRST_SWAP], arrived[FIRST_SWAP:])
    ]
    return tuple(
        pl.pallas_call(
            functools.partial(update_kernel, slots),
            out_shape=[jax.ShapeDtypeStruct(grads.shape, jnp.float32)] * 3
            + [jax.ShapeDtypeStruct(grads.shape, jnp.bfloat16)],
            in_specs=[smem, smem] + [vmem] * (len(ROUNDS) + 3),
            out_specs=[vmem] * 4,
            compiler_params=params,
        )(counts, new_layers, grads, *arrived, *swapped)
    )


def solution(mesh):
    placed = (
        P("section", "dp"),
        P("section", "dp"),
        P("section", "dp"),
        P(("section", "dp"), None),
        P(),
        P(),
        P(),
    )
    return jax.shard_map(
        on_device,
        mesh=mesh,
        in_specs=placed,
        out_specs=(
            P(("section", "dp"), None),
            P(("section", "dp"), None),
            P(("section", "dp"), None),
            P(("section", "dp"), None),
        ),
        check_vma=False,
    )
```

```python
import functools

import jax
import jax.numpy as jnp
from jax import lax
from jax.experimental import pallas as pl
from jax.experimental.pallas import tpu as pltpu
from jax.sharding import PartitionSpec as P

STEP = 1000
LANES = 128
SUBLANES = 8
AXES = ("section", "dp")
ROUNDS = ((0, 0), (2, 0), (0, 1), (2, 1), (1, 0), (3, 0), (1, 1), (3, 1))
PARAMS = pltpu.CompilerParams(vmem_limit_bytes=40 * 2**20)
ALONE = pltpu.CompilerParams(vmem_limit_bytes=62 * 2**20)


def target(old_section, block, shift, flip):
    z, core = old_section >> 1, old_section & 1
    y, x = block >> 2, block & 3
    turn = 2 * ((y + shift) & 3) + ((x & 1) ^ flip)
    odd = (z & 1) ^ core
    move = (turn + odd * (4 - 2 * turn)) * (1 - 2 * core)
    return 2 * ((z + move) & 7) + (core ^ (x >> 1))


def origin(old_section, new_section, shift, flip):
    z, core = old_section >> 1, old_section & 1
    move = ((new_section >> 1) - z) * (1 - 2 * core)
    odd = (z & 1) ^ core
    turn = (move + odd * (4 - 2 * move)) & 7
    y = ((turn >> 1) - shift) & 3
    x = 2 * (core ^ (new_section & 1)) + ((turn & 1) ^ flip)
    return 4 * y + x


def round_pairs(shift, flip):
    pairs = []
    for section in range(16):
        for rank in range(16):
            there = target(section, rank, shift, flip)
            pairs.append((section * 16 + rank, there * 16 + section))
    return pairs


SWAP = [(s * 16 + r, (s ^ 1) * 16 + r) for s in range(16) for r in range(16)]


def pack_kernel(slots, rounds, old_hbm, new_hbm, *refs):
    states, messages = refs[:3], refs[3 : 3 + len(rounds)]
    old_ref, new_ref, row_of, small_sem, state_sem = refs[3 + len(rounds) : 8 + len(rounds)]
    landed, tiles = refs[8 + len(rounds) : 11 + len(rounds)], refs[11 + len(rounds) :]
    section, rank = lax.axis_index("section"), lax.axis_index("dp")
    columns = states[0].shape[1] // LANES
    small = [
        pltpu.make_async_copy(old_hbm, old_ref, small_sem.at[0]),
        pltpu.make_async_copy(new_hbm, new_ref, small_sem.at[1]),
    ]
    large = []
    for index in range(3):
        for half in range(slots // SUBLANES):
            rows = pl.ds(half * SUBLANES, SUBLANES)
            large.append(
                pltpu.make_async_copy(
                    states[index].at[rows], landed[index].at[rows], state_sem.at[index, half]
                )
            )
    for copy in small + large:
        copy.start()
    for copy in small:
        copy.wait()
    for slot in range(slots):
        row_of[old_ref[section * slots + slot]] = slot
    for index in range(3):
        for half in range(slots // SUBLANES):
            large[index * (slots // SUBLANES) + half].wait()
            for column in range(columns):
                tiles[index][pl.ds((half * columns + column) * SUBLANES, SUBLANES), :] = landed[index][
                    pl.ds(half * SUBLANES, SUBLANES), pl.ds(column * LANES, LANES)
                ]
    for message, (shift, flip) in zip(messages, rounds):
        there = target(section, rank, shift, flip)
        for part in range(2):
            row = row_of[new_ref[(there ^ part) * slots + section]]
            start = (row >> 3) * (columns * SUBLANES) + (row & 7)
            for index, tile in enumerate(tiles):
                for half in range(2):
                    for column in range(8):
                        message[
                            pl.ds((part * 3 + index) * 16 + half * SUBLANES, SUBLANES),
                            pl.ds(column * LANES, LANES),
                        ] = tile[
                            pl.ds(start + (64 * half + column) * SUBLANES, SUBLANES, stride=64), :
                        ]


def pack(rounds, old_layers, new_layers, states):
    slots, columns = states[0].shape
    total = old_layers.shape[0]
    return pl.pallas_call(
        functools.partial(pack_kernel, slots, rounds),
        out_shape=[jax.ShapeDtypeStruct((96, 1024), jnp.float32)] * len(rounds),
        in_specs=[pl.BlockSpec(memory_space=pltpu.HBM)] * 5,
        out_specs=[pl.BlockSpec(memory_space=pltpu.VMEM)] * len(rounds),
        scratch_shapes=[pltpu.SMEM((total,), jnp.int32)] * 3
        + [pltpu.SemaphoreType.DMA((2,)), pltpu.SemaphoreType.DMA((3, slots // SUBLANES))]
        + [pltpu.VMEM((slots, columns), jnp.float32)] * 3
        + [pltpu.VMEM((slots * columns // LANES, LANES), jnp.float32)] * 3,
        compiler_params=ALONE,
        cost_estimate=pl.CostEstimate(flops=0, bytes_accessed=3 * 2**20, transcendentals=0),
    )(old_layers, new_layers, *states)


def adamw(weight, first, second, grad, live):
    first = 0.9 * first + 0.1 * grad
    second = 0.95 * second + 0.05 * grad * grad
    step_size = first / (1.0 - 0.9**STEP) / (jnp.sqrt(second / (1.0 - 0.95**STEP)) + 1e-08)
    weight = weight - 0.01 * (step_size + 0.1 * weight)
    zero = jnp.float32(0.0)
    return (
        jnp.where(live, weight, zero),
        jnp.where(live, first, zero),
        jnp.where(live, second, zero),
    )


def update_kernel(slots, rounds, packed, kept, counts_hbm, new_hbm, grads, *refs):
    count = 1 if packed else len(rounds)
    earlier = 0 if kept else 4
    held = refs[:count]
    outs = refs[count + earlier : count + earlier + 4]
    counts_ref, new_ref, small_sem, out_sem = refs[count + earlier + 4 : count + earlier + 8]
    done = refs[count + earlier + 8 :]
    section, rank = lax.axis_index("section"), lax.axis_index("dp")
    small = [
        pltpu.make_async_copy(counts_hbm, counts_ref, small_sem.at[0]),
        pltpu.make_async_copy(new_hbm, new_ref, small_sem.at[1]),
    ]
    for copy in small:
        copy.start()
    for copy in small:
        copy.wait()
    limit = counts_ref[new_ref[section * slots + rank]]
    width = grads.shape[1]
    place = width * lax.broadcasted_iota(jnp.int32, (16, width), 0) + lax.broadcasted_iota(
        jnp.int32, (16, width), 1
    )
    copies = []
    for number, (shift, flip) in enumerate(rounds):
        spot = origin(rank, section, shift, flip) ^ (0 if kept else 2)
        source = held[0].at[pl.ds(48 * number, 48)] if packed else held[number]
        rows = pl.ds(pl.multiple_of(spot * 16, 16), 16)
        live = place < limit - spot * (16 * width)
        results = adamw(
            source[pl.ds(0, 16), :], source[pl.ds(16, 16), :], source[pl.ds(32, 16), :], grads[rows, :], live
        )
        results = (*results, results[0].astype(jnp.bfloat16))
        for index, result in enumerate(results):
            done[index][pl.ds(number * 16, 16), :] = result
            copy = pltpu.make_async_copy(
                done[index].at[pl.ds(number * 16, 16)], outs[index].at[rows], out_sem.at[index, number]
            )
            copy.start()
            copies.append(copy)
    for copy in copies:
        copy.wait()


def update(rounds, counts, new_layers, grads, arrived, before):
    slots = 16
    hbm = pl.BlockSpec(memory_space=pltpu.HBM)
    vmem = pl.BlockSpec(memory_space=pltpu.VMEM)
    count = len(rounds)
    shapes = [jax.ShapeDtypeStruct(grads.shape, jnp.float32)] * 3 + [
        jax.ShapeDtypeStruct(grads.shape, jnp.bfloat16)
    ]
    return pl.pallas_call(
        functools.partial(update_kernel, slots, rounds, len(arrived) < count, not before),
        out_shape=shapes,
        in_specs=[hbm, hbm] + [vmem] * (len(arrived) + 1) + [hbm] * len(before),
        out_specs=[hbm] * 4,
        scratch_shapes=[pltpu.SMEM(counts.shape, jnp.int32)] * 2
        + [pltpu.SemaphoreType.DMA((2,)), pltpu.SemaphoreType.DMA((4, count))]
        + [pltpu.VMEM((16 * count, grads.shape[1]), shape.dtype) for shape in shapes],
        input_output_aliases={len(arrived) + 3 + i: i for i in range(len(before))},
        compiler_params=PARAMS,
        cost_estimate=pl.CostEstimate(
            flops=count * 2**20, bytes_accessed=count * 2**20, transcendentals=count * 2**16
        ),
    )(counts, new_layers, grads, *arrived, *before)


def on_device(master, momentum, variance, grads, counts, old_layers, new_layers):
    states = (master, momentum, variance)
    messages = pack(ROUNDS[:1], old_layers, new_layers, states) + pack(
        ROUNDS[1:], old_layers, new_layers, states
    )
    arrived = [
        lax.ppermute(message, AXES, round_pairs(*turn)) for message, turn in zip(messages, ROUNDS)
    ]
    swapped = lax.ppermute(jnp.concatenate([got[48:] for got in arrived]), AXES, SWAP)
    outs = update(ROUNDS, counts, new_layers, grads, arrived, ())
    return tuple(update(ROUNDS, counts, new_layers, grads, [swapped], outs))


def solution(mesh):
    placed = (
        P("section", "dp"),
        P("section", "dp"),
        P("section", "dp"),
        P(("section", "dp"), None),
        P(),
        P(),
        P(),
    )
    return jax.shard_map(
        on_device,
        mesh=mesh,
        in_specs=placed,
        out_specs=(
            P(("section", "dp"), None),
            P(("section", "dp"), None),
            P(("section", "dp"), None),
            P(("section", "dp"), None),
        ),
        check_vma=False,
    )
```

```python
import functools

import jax
import jax.numpy as jnp
from jax import lax
from jax.experimental import pallas as pl
from jax.experimental.pallas import tpu as pltpu
from jax.sharding import PartitionSpec as P

STEP = 1000
LANES = 128
SUBLANES = 8
AXES = ("section", "dp")
PACKS = ((0, 1), (2, 3, 4, 5, 6, 7))
SWAPS = ((0, 1), (2, 3), (4, 5), (6,), (7,))
UPDATES = (((0, 1, 2, 3, 4, 5), (0, 1, 2)), ((6, 7), (3, 4)))
ROUNDS = ((0, 0), (2, 0), (1, 1), (3, 1), (1, 0), (3, 0), (0, 1), (2, 1))
PARAMS = pltpu.CompilerParams(vmem_limit_bytes=40 * 2**20)
ALONE = pltpu.CompilerParams(vmem_limit_bytes=62 * 2**20)


def target(old_section, block, shift, flip):
    z, core = old_section >> 1, old_section & 1
    y, x = block >> 2, block & 3
    turn = 2 * ((y + shift) & 3) + ((x & 1) ^ flip)
    odd = (z & 1) ^ core
    move = (turn + odd * (4 - 2 * turn)) * (1 - 2 * core)
    return 2 * ((z + move) & 7) + (core ^ (x >> 1))


def origin(old_section, new_section, shift, flip):
    z, core = old_section >> 1, old_section & 1
    move = ((new_section >> 1) - z) * (1 - 2 * core)
    odd = (z & 1) ^ core
    turn = (move + odd * (4 - 2 * move)) & 7
    y = ((turn >> 1) - shift) & 3
    x = 2 * (core ^ (new_section & 1)) + ((turn & 1) ^ flip)
    return 4 * y + x


def round_pairs(shift, flip):
    pairs = []
    for section in range(16):
        for rank in range(16):
            there = target(section, rank, shift, flip)
            pairs.append((section * 16 + rank, there * 16 + section))
    return pairs


SWAP = [(s * 16 + r, (s ^ 1) * 16 + r) for s in range(16) for r in range(16)]


def pack_kernel(slots, rounds, old_hbm, new_hbm, *refs):
    states, messages = refs[:3], refs[3 : 3 + len(rounds)]
    old_ref, new_ref, row_of, small_sem, state_sem, out_sem, filled = refs[3 + len(rounds) : 10 + len(rounds)]
    landed, tiles = refs[10 + len(rounds) : 13 + len(rounds)], refs[13 + len(rounds) :]
    section, rank = lax.axis_index("section"), lax.axis_index("dp")
    columns = states[0].shape[1] // LANES
    small = [
        pltpu.make_async_copy(old_hbm, old_ref, small_sem.at[0]),
        pltpu.make_async_copy(new_hbm, new_ref, small_sem.at[1]),
    ]
    large = []
    for index in range(3):
        for half in range(slots // SUBLANES):
            rows = pl.ds(half * SUBLANES, SUBLANES)
            large.append(
                pltpu.make_async_copy(
                    states[index].at[rows], landed[index].at[rows], state_sem.at[index, half]
                )
            )
    for copy in small + large:
        copy.start()
    for copy in small:
        copy.wait()
    for slot in range(slots):
        row_of[old_ref[section * slots + slot]] = slot
    for index in range(3):
        for half in range(slots // SUBLANES):
            large[index * (slots // SUBLANES) + half].wait()
            for column in range(columns):
                tiles[index][pl.ds((half * columns + column) * SUBLANES, SUBLANES), :] = landed[index][
                    pl.ds(half * SUBLANES, SUBLANES), pl.ds(column * LANES, LANES)
                ]
    copies = []
    for number, (shift, flip) in enumerate(rounds):
        message = filled.at[number]
        there = target(section, rank, shift, flip)
        for part in range(2):
            row = row_of[new_ref[(there ^ part) * slots + section]]
            start = (row >> 3) * (columns * SUBLANES) + (row & 7)
            for index, tile in enumerate(tiles):
                for half in range(2):
                    for column in range(8):
                        message[
                            pl.ds((part * 3 + index) * 16 + half * SUBLANES, SUBLANES),
                            pl.ds(column * LANES, LANES),
                        ] = tile[
                            pl.ds(start + (64 * half + column) * SUBLANES, SUBLANES, stride=64), :
                        ]
        copy = pltpu.make_async_copy(message, messages[number], out_sem.at[number])
        copy.start()
        copies.append(copy)
    for copy in copies:
        copy.wait()


def pack(rounds, old_layers, new_layers, states):
    slots, columns = states[0].shape
    total = old_layers.shape[0]
    return pl.pallas_call(
        functools.partial(pack_kernel, slots, rounds),
        out_shape=[jax.ShapeDtypeStruct((96, 1024), jnp.float32)] * len(rounds),
        in_specs=[pl.BlockSpec(memory_space=pltpu.HBM)] * 5,
        out_specs=[pl.BlockSpec(memory_space=pltpu.HBM)] * len(rounds),
        scratch_shapes=[pltpu.SMEM((total,), jnp.int32)] * 3
        + [pltpu.SemaphoreType.DMA((2,)), pltpu.SemaphoreType.DMA((3, slots // SUBLANES))]
        + [pltpu.SemaphoreType.DMA((len(rounds),)), pltpu.VMEM((len(rounds), 96, 1024), jnp.float32)]
        + [pltpu.VMEM((slots, columns), jnp.float32)] * 3
        + [pltpu.VMEM((slots * columns // LANES, LANES), jnp.float32)] * 3,
        compiler_params=ALONE,
        cost_estimate=pl.CostEstimate(flops=0, bytes_accessed=3 * 2**20, transcendentals=0),
    )(old_layers, new_layers, *states)


def adamw(weight, first, second, grad, live):
    first = 0.9 * first + 0.1 * grad
    second = 0.95 * second + 0.05 * grad * grad
    step_size = first / (1.0 - 0.9**STEP) / (jnp.sqrt(second / (1.0 - 0.95**STEP)) + 1e-08)
    weight = weight - 0.01 * (step_size + 0.1 * weight)
    zero = jnp.float32(0.0)
    return (
        jnp.where(live, weight, zero),
        jnp.where(live, first, zero),
        jnp.where(live, second, zero),
    )


def update_kernel(slots, pieces, arrays, earlier, counts_hbm, new_hbm, grads, *refs):
    held = refs[:arrays]
    outs = refs[arrays + earlier : arrays + earlier + 4]
    counts_ref, new_ref, small_sem, out_sem = refs[arrays + earlier + 4 : arrays + earlier + 8]
    done = refs[arrays + earlier + 8 :]
    section, rank = lax.axis_index("section"), lax.axis_index("dp")
    small = [
        pltpu.make_async_copy(counts_hbm, counts_ref, small_sem.at[0]),
        pltpu.make_async_copy(new_hbm, new_ref, small_sem.at[1]),
    ]
    for copy in small:
        copy.start()
    for copy in small:
        copy.wait()
    limit = counts_ref[new_ref[section * slots + rank]]
    width = grads.shape[1]
    place = width * lax.broadcasted_iota(jnp.int32, (16, width), 0) + lax.broadcasted_iota(
        jnp.int32, (16, width), 1
    )
    copies = []
    for number, (array, offset, turn, kept) in enumerate(pieces):
        spot = origin(rank, section, *ROUNDS[turn]) ^ (0 if kept else 2)
        source = held[array].at[pl.ds(offset, 48)]
        rows = pl.ds(pl.multiple_of(spot * 16, 16), 16)
        live = place < limit - spot * (16 * width)
        results = adamw(
            source[pl.ds(0, 16), :], source[pl.ds(16, 16), :], source[pl.ds(32, 16), :], grads[rows, :], live
        )
        results = (*results, results[0].astype(jnp.bfloat16))
        for index, result in enumerate(results):
            done[index][pl.ds(number * 16, 16), :] = result
            copy = pltpu.make_async_copy(
                done[index].at[pl.ds(number * 16, 16)], outs[index].at[rows], out_sem.at[index, number]
            )
            copy.start()
            copies.append(copy)
    for copy in copies:
        copy.wait()


def update(kept, swapped, counts, new_layers, grads, arrived, exchanged, before):
    slots = 16
    arrays, pieces = [], []
    for turn in kept:
        pieces.append((len(arrays), 0, turn, True))
        arrays.append(arrived[turn])
    for group in swapped:
        for number, turn in enumerate(SWAPS[group]):
            pieces.append((len(arrays), 48 * number, turn, False))
        arrays.append(exchanged[group])
    count = len(pieces)
    hbm = pl.BlockSpec(memory_space=pltpu.HBM)
    vmem = pl.BlockSpec(memory_space=pltpu.VMEM)
    shapes = [jax.ShapeDtypeStruct(grads.shape, jnp.float32)] * 3 + [
        jax.ShapeDtypeStruct(grads.shape, jnp.bfloat16)
    ]
    return pl.pallas_call(
        functools.partial(update_kernel, slots, tuple(pieces), len(arrays), len(before)),
        out_shape=shapes,
        in_specs=[hbm, hbm] + [vmem] * (len(arrays) + 1) + [hbm] * len(before),
        out_specs=[hbm] * 4,
        scratch_shapes=[pltpu.SMEM(counts.shape, jnp.int32)] * 2
        + [pltpu.SemaphoreType.DMA((2,)), pltpu.SemaphoreType.DMA((4, count))]
        + [pltpu.VMEM((16 * count, grads.shape[1]), shape.dtype) for shape in shapes],
        input_output_aliases={len(arrays) + 3 + i: i for i in range(len(before))},
        compiler_params=PARAMS,
        cost_estimate=pl.CostEstimate(
            flops=count * 2**20, bytes_accessed=count * 2**19, transcendentals=count * 2**16
        ),
    )(counts, new_layers, grads, *arrays, *before)


def on_device(master, momentum, variance, grads, counts, old_layers, new_layers):
    states = (master, momentum, variance)
    messages = []
    for part in PACKS:
        if messages:
            old_layers, messages[-1] = lax.optimization_barrier((old_layers, messages[-1]))
        messages += pack(tuple(ROUNDS[turn] for turn in part), old_layers, new_layers, states)
    arrived = [
        lax.ppermute(message, AXES, round_pairs(*turn)) for message, turn in zip(messages, ROUNDS)
    ]
    exchanged = [
        lax.ppermute(jnp.concatenate([arrived[turn][48:] for turn in group]), AXES, SWAP)
        for group in SWAPS
    ]
    outs = ()
    for kept, swapped in UPDATES:
        outs = update(kept, swapped, counts, new_layers, grads, arrived, exchanged, outs)
    return tuple(outs)


def solution(mesh):
    placed = (
        P("section", "dp"),
        P("section", "dp"),
        P("section", "dp"),
        P(("section", "dp"), None),
        P(),
        P(),
        P(),
    )
    return jax.shard_map(
        on_device,
        mesh=mesh,
        in_specs=placed,
        out_specs=(
            P(("section", "dp"), None),
            P(("section", "dp"), None),
            P(("section", "dp"), None),
            P(("section", "dp"), None),
        ),
        check_vma=False,
    )
```

```python
import functools

import jax
import jax.numpy as jnp
from jax import lax
from jax.experimental import pallas as pl
from jax.experimental.pallas import tpu as pltpu
from jax.sharding import PartitionSpec as P

STEP = 1000
LANES = 128
SUBLANES = 8
AXES = ("section", "dp")
PACKS = ((0, 1), (2, 3, 4, 5, 6, 7))
SWAPS = ((0, 1), (2, 3), (4, 5), (6,), (7,))
ROUNDS = ((0, 0), (2, 0), (1, 1), (3, 1), (1, 0), (3, 0), (0, 1), (2, 1))
PARAMS = pltpu.CompilerParams(vmem_limit_bytes=40 * 2**20)
ALONE = pltpu.CompilerParams(vmem_limit_bytes=62 * 2**20)


def target(old_section, block, shift, flip):
    z, core = old_section >> 1, old_section & 1
    y, x = block >> 2, block & 3
    turn = 2 * ((y + shift) & 3) + ((x & 1) ^ flip)
    odd = (z & 1) ^ core
    move = (turn + odd * (4 - 2 * turn)) * (1 - 2 * core)
    return 2 * ((z + move) & 7) + (core ^ (x >> 1))


def origin(old_section, new_section, shift, flip):
    z, core = old_section >> 1, old_section & 1
    move = ((new_section >> 1) - z) * (1 - 2 * core)
    odd = (z & 1) ^ core
    turn = (move + odd * (4 - 2 * move)) & 7
    y = ((turn >> 1) - shift) & 3
    x = 2 * (core ^ (new_section & 1)) + ((turn & 1) ^ flip)
    return 4 * y + x


def round_pairs(shift, flip):
    pairs = []
    for section in range(16):
        for rank in range(16):
            there = target(section, rank, shift, flip)
            pairs.append((section * 16 + rank, there * 16 + section))
    return pairs


SWAP = [(s * 16 + r, (s ^ 1) * 16 + r) for s in range(16) for r in range(16)]


def pack_kernel(slots, rounds, old_hbm, new_hbm, *refs):
    states, messages = refs[:3], refs[3 : 3 + len(rounds)]
    old_ref, new_ref, row_of, small_sem, state_sem, out_sem, filled = refs[3 + len(rounds) : 10 + len(rounds)]
    landed, tiles = refs[10 + len(rounds) : 13 + len(rounds)], refs[13 + len(rounds) :]
    section, rank = lax.axis_index("section"), lax.axis_index("dp")
    columns = states[0].shape[1] // LANES
    small = [
        pltpu.make_async_copy(old_hbm, old_ref, small_sem.at[0]),
        pltpu.make_async_copy(new_hbm, new_ref, small_sem.at[1]),
    ]
    large = []
    for index in range(3):
        for half in range(slots // SUBLANES):
            rows = pl.ds(half * SUBLANES, SUBLANES)
            large.append(
                pltpu.make_async_copy(
                    states[index].at[rows], landed[index].at[rows], state_sem.at[index, half]
                )
            )
    for copy in small + large:
        copy.start()
    for copy in small:
        copy.wait()
    for slot in range(slots):
        row_of[old_ref[section * slots + slot]] = slot
    for index in range(3):
        for half in range(slots // SUBLANES):
            large[index * (slots // SUBLANES) + half].wait()
            for column in range(columns):
                tiles[index][pl.ds((half * columns + column) * SUBLANES, SUBLANES), :] = landed[index][
                    pl.ds(half * SUBLANES, SUBLANES), pl.ds(column * LANES, LANES)
                ]
    copies = []
    for number, (shift, flip) in enumerate(rounds):
        message = filled.at[number]
        there = target(section, rank, shift, flip)
        for part in range(2):
            row = row_of[new_ref[(there ^ part) * slots + section]]
            start = (row >> 3) * (columns * SUBLANES) + (row & 7)
            for index, tile in enumerate(tiles):
                for half in range(2):
                    for column in range(8):
                        message[
                            pl.ds((part * 3 + index) * 16 + half * SUBLANES, SUBLANES),
                            pl.ds(column * LANES, LANES),
                        ] = tile[
                            pl.ds(start + (64 * half + column) * SUBLANES, SUBLANES, stride=64), :
                        ]
        copy = pltpu.make_async_copy(message, messages[number], out_sem.at[number])
        copy.start()
        copies.append(copy)
    for copy in copies:
        copy.wait()


def pack(rounds, old_layers, new_layers, states):
    slots, columns = states[0].shape
    total = old_layers.shape[0]
    return pl.pallas_call(
        functools.partial(pack_kernel, slots, rounds),
        out_shape=[jax.ShapeDtypeStruct((96, 1024), jnp.float32)] * len(rounds),
        in_specs=[pl.BlockSpec(memory_space=pltpu.HBM)] * 5,
        out_specs=[pl.BlockSpec(memory_space=pltpu.HBM)] * len(rounds),
        scratch_shapes=[pltpu.SMEM((total,), jnp.int32)] * 3
        + [pltpu.SemaphoreType.DMA((2,)), pltpu.SemaphoreType.DMA((3, slots // SUBLANES))]
        + [pltpu.SemaphoreType.DMA((len(rounds),)), pltpu.VMEM((len(rounds), 96, 1024), jnp.float32)]
        + [pltpu.VMEM((slots, columns), jnp.float32)] * 3
        + [pltpu.VMEM((slots * columns // LANES, LANES), jnp.float32)] * 3,
        compiler_params=ALONE,
        cost_estimate=pl.CostEstimate(flops=0, bytes_accessed=3 * 2**20, transcendentals=0),
    )(old_layers, new_layers, *states)


def adamw(weight, first, second, grad, live):
    first = 0.9 * first + 0.1 * grad
    second = 0.95 * second + 0.05 * grad * grad
    step_size = first / (1.0 - 0.9**STEP) / (jnp.sqrt(second / (1.0 - 0.95**STEP)) + 1e-08)
    weight = weight - 0.01 * (step_size + 0.1 * weight)
    zero = jnp.float32(0.0)
    return (
        jnp.where(live, weight, zero),
        jnp.where(live, first, zero),
        jnp.where(live, second, zero),
    )


def update_kernel(slots, pieces, arrays, counts_hbm, new_hbm, grads, *refs):
    held = refs[:arrays]
    outs = refs[arrays : arrays + 4]
    counts_ref, new_ref, small_sem, out_sem = refs[arrays + 4 : arrays + 8]
    done = refs[arrays + 8 :]
    section, rank = lax.axis_index("section"), lax.axis_index("dp")
    small = [
        pltpu.make_async_copy(counts_hbm, counts_ref, small_sem.at[0]),
        pltpu.make_async_copy(new_hbm, new_ref, small_sem.at[1]),
    ]
    for copy in small:
        copy.start()
    for copy in small:
        copy.wait()
    limit = counts_ref[new_ref[section * slots + rank]]
    width = grads.shape[1]
    place = width * lax.broadcasted_iota(jnp.int32, (16, width), 0) + lax.broadcasted_iota(
        jnp.int32, (16, width), 1
    )
    copies = []
    for number, (array, offset, turn, kept) in enumerate(pieces):
        spot = origin(rank, section, *ROUNDS[turn]) ^ (0 if kept else 2)
        source = held[array].at[pl.ds(offset, 48)]
        rows = pl.ds(pl.multiple_of(spot * 16, 16), 16)
        live = place < limit - spot * (16 * width)
        results = adamw(
            source[pl.ds(0, 16), :], source[pl.ds(16, 16), :], source[pl.ds(32, 16), :], grads[rows, :], live
        )
        results = (*results, results[0].astype(jnp.bfloat16))
        for index, result in enumerate(results):
            done[index][pl.ds(number * 16, 16), :] = result
            copy = pltpu.make_async_copy(
                done[index].at[pl.ds(number * 16, 16)], outs[index].at[rows], out_sem.at[index, number]
            )
            copy.start()
            copies.append(copy)
    for copy in copies:
        copy.wait()


def update(slots, counts, new_layers, grads, arrived, exchanged):
    arrays, pieces = [], []
    for turn, got in enumerate(arrived):
        pieces.append((len(arrays), 0, turn, True))
        arrays.append(got)
    for group, got in zip(SWAPS, exchanged):
        for number, turn in enumerate(group):
            pieces.append((len(arrays), 48 * number, turn, False))
        arrays.append(got)
    count = len(pieces)
    hbm = pl.BlockSpec(memory_space=pltpu.HBM)
    vmem = pl.BlockSpec(memory_space=pltpu.VMEM)
    shapes = [jax.ShapeDtypeStruct(grads.shape, jnp.float32)] * 3 + [
        jax.ShapeDtypeStruct(grads.shape, jnp.bfloat16)
    ]
    return pl.pallas_call(
        functools.partial(update_kernel, slots, tuple(pieces), len(arrays)),
        out_shape=shapes,
        in_specs=[hbm, hbm] + [vmem] * (len(arrays) + 1),
        out_specs=[hbm] * 4,
        scratch_shapes=[pltpu.SMEM(counts.shape, jnp.int32)] * 2
        + [pltpu.SemaphoreType.DMA((2,)), pltpu.SemaphoreType.DMA((4, count))]
        + [pltpu.VMEM((16 * count, grads.shape[1]), shape.dtype) for shape in shapes],
        compiler_params=PARAMS,
        cost_estimate=pl.CostEstimate(
            flops=count * 2**20, bytes_accessed=count * 2**19, transcendentals=count * 2**16
        ),
    )(counts, new_layers, grads, *arrays)


def on_device(master, momentum, variance, grads, counts, old_layers, new_layers):
    states = (master, momentum, variance)
    messages = []
    for part in PACKS:
        if messages:
            old_layers, messages[-1] = lax.optimization_barrier((old_layers, messages[-1]))
        messages += pack(tuple(ROUNDS[turn] for turn in part), old_layers, new_layers, states)
    arrived = [
        lax.ppermute(message, AXES, round_pairs(*turn)) for message, turn in zip(messages, ROUNDS)
    ]
    exchanged = [
        lax.ppermute(jnp.concatenate([arrived[turn][48:] for turn in group]), AXES, SWAP)
        for group in SWAPS
    ]
    return tuple(update(master.shape[0], counts, new_layers, grads, arrived, exchanged))


def solution(mesh):
    placed = (
        P("section", "dp"),
        P("section", "dp"),
        P("section", "dp"),
        P(("section", "dp"), None),
        P(),
        P(),
        P(),
    )
    return jax.shard_map(
        on_device,
        mesh=mesh,
        in_specs=placed,
        out_specs=(
            P(("section", "dp"), None),
            P(("section", "dp"), None),
            P(("section", "dp"), None),
            P(("section", "dp"), None),
        ),
        check_vma=False,
    )
```

```python
import functools

import jax
import jax.numpy as jnp
from jax import lax
from jax.experimental import pallas as pl
from jax.experimental.pallas import tpu as pltpu
from jax.sharding import PartitionSpec as P

STEP = 1000
LANES = 128
SUBLANES = 8
AXES = ("section", "dp")
PACKS = ((0, 1), (2, 3, 4, 5, 6, 7))
SWAPS = ((0, 1), (2, 3), (4, 5), (6,), (7,))
UPDATES = (((0, 1, 2, 3, 4, 5), (0, 1, 2)), ((6, 7), (3, 4)))
ROUNDS = ((0, 0), (2, 0), (1, 1), (3, 1), (1, 0), (3, 0), (0, 1), (2, 1))
EARLY = 4
PARAMS = pltpu.CompilerParams(vmem_limit_bytes=40 * 2**20)
ALONE = pltpu.CompilerParams(vmem_limit_bytes=62 * 2**20)


def target(old_section, block, shift, flip):
    z, core = old_section >> 1, old_section & 1
    y, x = block >> 2, block & 3
    turn = 2 * ((y + shift) & 3) + ((x & 1) ^ flip)
    odd = (z & 1) ^ core
    move = (turn + odd * (4 - 2 * turn)) * (1 - 2 * core)
    return 2 * ((z + move) & 7) + (core ^ (x >> 1))


def origin(old_section, new_section, shift, flip):
    z, core = old_section >> 1, old_section & 1
    move = ((new_section >> 1) - z) * (1 - 2 * core)
    odd = (z & 1) ^ core
    turn = (move + odd * (4 - 2 * move)) & 7
    y = ((turn >> 1) - shift) & 3
    x = 2 * (core ^ (new_section & 1)) + ((turn & 1) ^ flip)
    return 4 * y + x


def round_pairs(shift, flip):
    pairs = []
    for section in range(16):
        for rank in range(16):
            there = target(section, rank, shift, flip)
            pairs.append((section * 16 + rank, there * 16 + section))
    return pairs


SWAP = [(s * 16 + r, (s ^ 1) * 16 + r) for s in range(16) for r in range(16)]


def pack_kernel(slots, rounds, old_hbm, new_hbm, *refs):
    states, messages = refs[:3], refs[3 : 3 + len(rounds)]
    old_ref, new_ref, row_of, small_sem, state_sem, out_sem, filled = refs[3 + len(rounds) : 10 + len(rounds)]
    landed, tiles = refs[10 + len(rounds) : 13 + len(rounds)], refs[13 + len(rounds) :]
    section, rank = lax.axis_index("section"), lax.axis_index("dp")
    columns = states[0].shape[1] // LANES
    small = [
        pltpu.make_async_copy(old_hbm, old_ref, small_sem.at[0]),
        pltpu.make_async_copy(new_hbm, new_ref, small_sem.at[1]),
    ]
    large = []
    for index in range(3):
        for half in range(slots // SUBLANES):
            rows = pl.ds(half * SUBLANES, SUBLANES)
            large.append(
                pltpu.make_async_copy(
                    states[index].at[rows], landed[index].at[rows], state_sem.at[index, half]
                )
            )
    for copy in small + large:
        copy.start()
    for copy in small:
        copy.wait()
    for slot in range(slots):
        row_of[old_ref[section * slots + slot]] = slot
    for index in range(3):
        for half in range(slots // SUBLANES):
            large[index * (slots // SUBLANES) + half].wait()
            for column in range(columns):
                tiles[index][pl.ds((half * columns + column) * SUBLANES, SUBLANES), :] = landed[index][
                    pl.ds(half * SUBLANES, SUBLANES), pl.ds(column * LANES, LANES)
                ]
    copies = []
    for number, (shift, flip) in enumerate(rounds):
        message = filled.at[number]
        there = target(section, rank, shift, flip)
        for part in range(2):
            row = row_of[new_ref[(there ^ part) * slots + section]]
            start = (row >> 3) * (columns * SUBLANES) + (row & 7)
            for index, tile in enumerate(tiles):
                for half in range(2):
                    for column in range(8):
                        message[
                            pl.ds((part * 3 + index) * 16 + half * SUBLANES, SUBLANES),
                            pl.ds(column * LANES, LANES),
                        ] = tile[
                            pl.ds(start + (64 * half + column) * SUBLANES, SUBLANES, stride=64), :
                        ]
        copy = pltpu.make_async_copy(message, messages[number], out_sem.at[number])
        copy.start()
        copies.append(copy)
    for copy in copies:
        copy.wait()


def pack(rounds, old_layers, new_layers, states):
    slots, columns = states[0].shape
    total = old_layers.shape[0]
    return pl.pallas_call(
        functools.partial(pack_kernel, slots, rounds),
        out_shape=[jax.ShapeDtypeStruct((96, 1024), jnp.float32)] * len(rounds),
        in_specs=[pl.BlockSpec(memory_space=pltpu.HBM)] * 5,
        out_specs=[pl.BlockSpec(memory_space=pltpu.HBM)] * len(rounds),
        scratch_shapes=[pltpu.SMEM((total,), jnp.int32)] * 3
        + [pltpu.SemaphoreType.DMA((2,)), pltpu.SemaphoreType.DMA((3, slots // SUBLANES))]
        + [pltpu.SemaphoreType.DMA((len(rounds),)), pltpu.VMEM((len(rounds), 96, 1024), jnp.float32)]
        + [pltpu.VMEM((slots, columns), jnp.float32)] * 3
        + [pltpu.VMEM((slots * columns // LANES, LANES), jnp.float32)] * 3,
        compiler_params=ALONE,
        cost_estimate=pl.CostEstimate(flops=0, bytes_accessed=3 * 2**20, transcendentals=0),
    )(old_layers, new_layers, *states)


def adamw(weight, first, second, grad):
    first = 0.9 * first + 0.1 * grad
    second = 0.95 * second + 0.05 * grad * grad
    step_size = first / (1.0 - 0.9**STEP) / (jnp.sqrt(second / (1.0 - 0.95**STEP)) + 1e-08)
    weight = weight - 0.01 * (step_size + 0.1 * weight)
    return weight, first, second


def update_kernel(slots, pieces, arrays, earlier, counts_hbm, new_hbm, grads, *refs):
    held = refs[:arrays]
    outs = refs[arrays + earlier : arrays + earlier + 4]
    counts_ref, new_ref, small_sem, out_sem = refs[arrays + earlier + 4 : arrays + earlier + 8]
    done = refs[arrays + earlier + 8 :]
    section, rank = lax.axis_index("section"), lax.axis_index("dp")
    small = [
        pltpu.make_async_copy(counts_hbm, counts_ref, small_sem.at[0]),
        pltpu.make_async_copy(new_hbm, new_ref, small_sem.at[1]),
    ]
    for copy in small:
        copy.start()
    for number, (array, offset, turn, kept) in enumerate(pieces[:EARLY]):
        spot = origin(rank, section, *ROUNDS[turn]) ^ (0 if kept else 2)
        source = held[array].at[pl.ds(offset, 48)]
        rows = pl.ds(pl.multiple_of(spot * 16, 16), 16)
        results = adamw(source[pl.ds(0, 16), :], source[pl.ds(16, 16), :], source[pl.ds(32, 16), :], grads[rows, :])
        for index, result in enumerate(results):
            done[index][pl.ds(number * 16, 16), :] = result
    for copy in small:
        copy.wait()
    limit = counts_ref[new_ref[section * slots + rank]]
    width = grads.shape[1]
    place = width * lax.broadcasted_iota(jnp.int32, (16, width), 0) + lax.broadcasted_iota(
        jnp.int32, (16, width), 1
    )
    copies = []
    for number, (array, offset, turn, kept) in enumerate(pieces):
        spot = origin(rank, section, *ROUNDS[turn]) ^ (0 if kept else 2)
        source = held[array].at[pl.ds(offset, 48)]
        rows = pl.ds(pl.multiple_of(spot * 16, 16), 16)
        live = place < limit - spot * (16 * width)
        if number < EARLY:
            results = [done[index][pl.ds(number * 16, 16), :] for index in range(3)]
        else:
            results = adamw(
                source[pl.ds(0, 16), :], source[pl.ds(16, 16), :], source[pl.ds(32, 16), :], grads[rows, :]
            )
        results = [jnp.where(live, result, jnp.float32(0.0)) for result in results]
        results.append(results[0].astype(jnp.bfloat16))
        for index, result in enumerate(results):
            done[index][pl.ds(number * 16, 16), :] = result
            copy = pltpu.make_async_copy(
                done[index].at[pl.ds(number * 16, 16)], outs[index].at[rows], out_sem.at[index, number]
            )
            copy.start()
            copies.append(copy)
    for copy in copies:
        copy.wait()


def update(kept, swapped, counts, new_layers, grads, arrived, exchanged, before):
    slots = 16
    arrays, pieces = [], []
    for turn in kept:
        pieces.append((len(arrays), 0, turn, True))
        arrays.append(arrived[turn])
    for group in swapped:
        for number, turn in enumerate(SWAPS[group]):
            pieces.append((len(arrays), 48 * number, turn, False))
        arrays.append(exchanged[group])
    count = len(pieces)
    hbm = pl.BlockSpec(memory_space=pltpu.HBM)
    vmem = pl.BlockSpec(memory_space=pltpu.VMEM)
    shapes = [jax.ShapeDtypeStruct(grads.shape, jnp.float32)] * 3 + [
        jax.ShapeDtypeStruct(grads.shape, jnp.bfloat16)
    ]
    return pl.pallas_call(
        functools.partial(update_kernel, slots, tuple(pieces), len(arrays), len(before)),
        out_shape=shapes,
        in_specs=[hbm, hbm] + [vmem] * (len(arrays) + 1) + [hbm] * len(before),
        out_specs=[hbm] * 4,
        scratch_shapes=[pltpu.SMEM(counts.shape, jnp.int32)] * 2
        + [pltpu.SemaphoreType.DMA((2,)), pltpu.SemaphoreType.DMA((4, count))]
        + [pltpu.VMEM((16 * count, grads.shape[1]), shape.dtype) for shape in shapes],
        input_output_aliases={len(arrays) + 3 + i: i for i in range(len(before))},
        compiler_params=PARAMS,
        cost_estimate=pl.CostEstimate(
            flops=count * 2**20, bytes_accessed=count * 2**19, transcendentals=count * 2**16
        ),
    )(counts, new_layers, grads, *arrays, *before)


def on_device(master, momentum, variance, grads, counts, old_layers, new_layers):
    states = (master, momentum, variance)
    messages = []
    for part in PACKS:
        if messages:
            old_layers, messages[-1] = lax.optimization_barrier((old_layers, messages[-1]))
        messages += pack(tuple(ROUNDS[turn] for turn in part), old_layers, new_layers, states)
    arrived = [
        lax.ppermute(message, AXES, round_pairs(*turn)) for message, turn in zip(messages, ROUNDS)
    ]
    exchanged = [
        lax.ppermute(jnp.concatenate([arrived[turn][48:] for turn in group]), AXES, SWAP)
        for group in SWAPS
    ]
    outs = ()
    for kept, swapped in UPDATES:
        outs = update(kept, swapped, counts, new_layers, grads, arrived, exchanged, outs)
    return tuple(outs)


def solution(mesh):
    placed = (
        P("section", "dp"),
        P("section", "dp"),
        P("section", "dp"),
        P(("section", "dp"), None),
        P(),
        P(),
        P(),
    )
    return jax.shard_map(
        on_device,
        mesh=mesh,
        in_specs=placed,
        out_specs=(
            P(("section", "dp"), None),
            P(("section", "dp"), None),
            P(("section", "dp"), None),
            P(("section", "dp"), None),
        ),
        check_vma=False,
    )
```
